32 devices in a mesh: dom: 8 (over z, x), grp: 4 (over y, core).
Axes of the slice: x: 2, y: 2, z: 4, core: 2. Of those that a mesh axis runs over, the one named last changes fastest.
Arguments:
- blocks: bfloat16 [1536, 6, 128, 128], P(('dom', 'grp')), may hold values from -0.21875 to 0.21875
- local_cols: int32 [1536, 4], P(('dom', 'grp')), may hold values from 0 to 191
- remote_refs: int32 [1536, 2], P(('dom', 'grp')), may hold values from 0 to 23
- send_blocks: int32 [8, 4, 8, 3], P('dom', 'grp'), may hold values from 0 to 47
- send_counts: int32 [8, 4, 8], P('dom', 'grp'), may hold values from 0 to 3
- probes: bfloat16 [64, 196608], P(None, ('dom', 'grp')), may hold values from -6 to 6
Outputs:
- moments: float32 [3, 196608], P(None, ('dom', 'grp'))
The draws below stay inside these ranges and needn't reach their ends.
All inputs are finite; a program needn't handle non-finite values.
Results may differ from the reference program's by a relative error of at most 0.00064.
Values may be sent and summed in bfloat16 or wider, within the bound.
A program may use at most 64 MiB of HBM per device.

```python
import math
import jax
import jax.numpy as jnp
from jax import lax

BS = 128
PROBES = 64
BR_DEV = 48
LOCAL = 4
REMOTE = 2
CAP = 3
KMOM = 256
PARTS_SIZE = 8
LANES = 4
BR_PART = 192
NB = 1536
NODES = 196608
SLOTS = 24
NNZ = 6


def touch_ends(entries, key, least, high):
    longest = entries.shape.index(max(entries.shape))
    spots = []
    for shift in (0, 1):
        where = [jax.random.randint(jax.random.fold_in(key, axis), (), 0, length) for axis, length in enumerate(entries.shape)]
        where[longest] = (where[longest] + shift) % entries.shape[longest]
        spots.append(tuple(where))
    return entries.at[spots[0]].set(least).at[spots[1]].set(high)


def steps_of(key, extent, shards, least, top_value):
    loudness = 1.0
    for axis_at, blocks in shards:
        draws = jax.random.uniform(jax.random.fold_in(jax.random.fold_in(key, 6), axis_at), (blocks,), jnp.float32, least / len(shards), top_value / len(shards))
        loudness = loudness * jnp.repeat(jnp.exp(draws), extent[axis_at] // blocks).reshape((-1,) + (1,) * (len(extent) - 1 - axis_at))
    return loudness


def noise(own_key, extent, deviation, most, shards=(), kind=jnp.bfloat16):
    drawn = jax.random.normal(own_key, extent, jnp.float32) * deviation
    if len(shards) > 0:
        drawn = steps_of(own_key, extent, shards, -0.22, 0.18) * drawn
    return jnp.clip(drawn, min=-most, max=most).astype(kind)


def setup_inputs(seed: int = 0) -> dict:
    seeds = jax.random.split(jax.random.key(seed), 7)
    return {
        "blocks": noise(seeds[0], (NB, NNZ, BS, BS), (NNZ * BS) ** -0.5, 0.21875, ((0, 32),)),
        "local_cols": touch_ends(jax.random.randint(seeds[1], (NB, LOCAL), 0, BR_PART), jax.random.fold_in(seeds[1], 1), 0, BR_PART - 1).astype(jnp.int32),
        "remote_refs": touch_ends(jax.random.randint(seeds[2], (NB, REMOTE), 0, SLOTS), jax.random.fold_in(seeds[2], 1), 0, SLOTS - 1).astype(jnp.int32),
        "send_blocks": touch_ends(jax.random.randint(seeds[3], (PARTS_SIZE, LANES, PARTS_SIZE, CAP), 0, BR_DEV), jax.random.fold_in(seeds[3], 1), 0, BR_DEV - 1).astype(jnp.int32),
        "send_counts": touch_ends(jax.random.randint(seeds[4], (PARTS_SIZE, LANES, PARTS_SIZE), 0, CAP + 1), jax.random.fold_in(seeds[4], 1), 0, CAP).astype(jnp.int32),
        "probes": noise(seeds[5], (PROBES, NODES), 1.0, 6.0, ((1, 32),)),
    }


def jackson(order, total):
    angle = math.pi / (total + 1)
    return ((total - order + 1) * math.cos(order * angle) + math.sin(order * angle) / math.tan(angle)) / (total + 1)

def reference(blocks, local_cols, remote_refs, send_blocks, send_counts, probes):
    rows = jnp.arange(NB, dtype=jnp.int32)
    part = rows // BR_PART
    lane = rows // BR_DEV % LANES
    local_global = part[:, None] * BR_PART + local_cols
    peer = remote_refs // CAP
    slot = remote_refs % CAP
    source = send_blocks[peer, lane[:, None], part[:, None], slot]
    remote_global = peer * BR_PART + lane[:, None] * BR_DEV + source
    live = (slot < send_counts[peer, lane[:, None], part[:, None]]).astype(jnp.float32)
    columns = jnp.concatenate([local_global.astype(jnp.int32), remote_global.astype(jnp.int32)], axis=1).astype(jnp.int32)
    weights = jnp.concatenate([jnp.ones((NB, LOCAL), jnp.float32), live], axis=1).astype(jnp.float32)
    groups = PARTS_SIZE * LANES
    grouped_blocks = blocks.reshape(groups, BR_DEV, NNZ, BS, BS)
    grouped_cols = columns.reshape(groups, BR_DEV, NNZ)
    grouped_weights = weights.reshape(groups, BR_DEV, NNZ)

    def apply_op(field):
        field_blocks = field.reshape(PROBES, NB, BS)

        def one_group(items):
            block_set, col_set, weight_set = items
            picked = jnp.take(field_blocks, col_set, axis=1).astype(jnp.float32)
            picked = picked * weight_set[None, :, :, None]
            return jnp.einsum('rjab,prjb->pra', block_set.astype(jnp.float32), picked)
        result = lax.map(one_group, (grouped_blocks, grouped_cols, grouped_weights))
        return jnp.transpose(result, (1, 0, 2, 3)).reshape(PROBES, NODES)
    first = apply_op(probes).astype(jnp.bfloat16)
    second = 2.0 * apply_op(first) - probes.astype(jnp.float32)
    base = probes.astype(jnp.float32)
    norm = 1.0 / math.sqrt(PROBES)
    moment_zero = jackson(0, KMOM) * norm * lax.optimization_barrier(jnp.sum(base * base, axis=0))
    moment_one = 2.0 * jackson(1, KMOM) * norm * lax.optimization_barrier(jnp.sum(base * first.astype(jnp.float32), axis=0))
    moment_two = 2.0 * jackson(2, KMOM) * norm * lax.optimization_barrier(jnp.sum(base * second, axis=0))
    return jnp.stack([moment_zero, moment_one, moment_two], axis=0)
```

```python
import functools
import math

import jax
import jax.numpy as jnp
from jax import lax
from jax.experimental import pallas as pl
from jax.experimental.pallas import tpu as pltpu
from jax.sharding import PartitionSpec as P

KMOM = 256
MESH = pl.DeviceIdType.MESH


def jackson(order, total):
    angle = math.pi / (total + 1)
    return (
        (total - order + 1) * math.cos(order * angle) + math.sin(order * angle) / math.tan(angle)
    ) / (total + 1)


def kernel(
    doms, lanes, chunks, scales,
    cols, refs, send_blocks, send_counts, probes, blocks, moments,
    weights, own_a, own_b, gathered_a, gathered_b, outgoing, received_a, received_b,
    load_sem, across_send, across_recv, pair_send, pair_recv, pass_send, pass_recv, edge_send, edge_recv,
):
    own, gathered, received = (own_a, own_b), (gathered_a, gathered_b), (received_a, received_b)
    rows, _, bs = own_a.shape
    local = cols.shape[0]
    remote = refs.shape[0]
    cap = send_blocks.shape[0]
    part = rows // chunks
    hops = lanes // 2 - 1
    d = lax.axis_index("dom")
    g = lax.axis_index("grp")
    pair = g + 1 - 2 * lax.rem(g, 2)

    def load(k):
        span = pl.ds(k * part, part)
        return pltpu.make_async_copy(blocks.at[span], weights.at[span], load_sem.at[k])

    barrier = pltpu.get_barrier_semaphore()
    for hop in range(1, lanes):
        pl.semaphore_signal(barrier, inc=1, device_id=(d, lax.rem(g + hop, lanes)), device_id_type=MESH)

    @pl.loop(1, doms)
    def _(k):
        pl.semaphore_signal(barrier, inc=1, device_id=(lax.rem(d + k, doms), g), device_id_type=MESH)

    for k in range(chunks):
        load(k).start()

    def across(phase, hop, k):
        to = lax.rem(g + 2 * hop, lanes)
        return pltpu.make_async_remote_copy(
            own[phase].at[pl.ds(k * part, part)],
            gathered[phase].at[pl.ds(g * rows + k * part, part)],
            across_send.at[phase, hop - 1, k], across_recv.at[phase, hop - 1, k],
            device_id=(d, to), device_id_type=MESH,
        )

    def to_pair(phase, k):
        return pltpu.make_async_remote_copy(
            own[phase].at[pl.ds(k * part, part)],
            gathered[phase].at[pl.ds(g * rows + k * part, part)],
            pair_send.at[phase, k], pair_recv.at[phase, k],
            device_id=(d, pair), device_id_type=MESH,
        )

    def pass_on(phase, hop, k):
        origin = lax.rem(g - 2 * hop + lanes, lanes)
        span = pl.ds(origin * rows + k * part, part)
        return pltpu.make_async_remote_copy(
            gathered[phase].at[span], gathered[phase].at[span],
            pass_send.at[phase, hop - 1, k], pass_recv.at[phase, hop - 1, k],
            device_id=(d, pair), device_id_type=MESH,
        )

    def edge(phase, k):
        to = lax.rem(d + k, doms)
        return pltpu.make_async_remote_copy(
            outgoing.at[phase, pl.ds(to * cap, cap)],
            received[phase].at[pl.ds(d * cap, cap)],
            edge_send.at[phase, k], edge_recv.at[phase, k],
            device_id=(to, g), device_id_type=MESH,
        )

    def send_chunk(phase, k):
        for hop in range(1, hops + 1):
            across(phase, hop, k).start()
        to_pair(phase, k).start()

    def send_edges(phase):
        def packed(to, s):
            block = own[phase][send_blocks[s, to]]
            return jnp.where(s < send_counts[0, to], block, jnp.zeros_like(block))

        @pl.loop(1, doms)
        def _(k):
            to = lax.rem(d + k, doms)
            for s in range(cap):
                outgoing[phase, to * cap + s] = packed(to, s)
            edge(phase, k).start()

        for s in range(cap):
            received[phase][d * cap + s] = packed(d, s)

    def finish_exchange(phase):
        for k in range(chunks):
            for hop in range(1, hops + 1):
                across(phase, hop, k).wait_recv()
                pass_on(phase, hop, k).start()
        for k in range(chunks):
            to_pair(phase, k).wait_recv()

        @pl.loop(1, doms)
        def _(k):
            edge(phase, k).wait_recv()

        for k in range(chunks):
            for hop in range(1, hops + 1):
                pass_on(phase, hop, k).wait_recv()

    def drain(phase):
        for k in range(chunks):
            for hop in range(1, hops + 1):
                across(phase, hop, k).wait_send()
                pass_on(phase, hop, k).wait_send()
            to_pair(phase, k).wait_send()

        @pl.loop(1, doms)
        def _(k):
            edge(phase, k).wait_send()

    def product(phase, r):
        picked = [gathered[phase][cols[j, r]] for j in range(local)]
        picked += [received[phase][refs[j, r]] for j in range(remote)]
        held = [weights[r, j] for j in range(local + remote)]
        return lax.dot_general(
            jnp.concatenate(picked, axis=1), jnp.concatenate(held, axis=1),
            (((1,), (1,)), ((), ())), preferred_element_type=jnp.float32,
        )

    for r in range(rows):
        block = probes[:, pl.ds(r * bs, bs)]
        own[0][r] = block
        gathered[0][g * rows + r] = block

    pl.semaphore_wait(barrier, lanes - 1 + doms - 1)
    for k in range(chunks):
        send_chunk(0, k)
    send_edges(0)

    for r in range(rows):
        base = own[0][r].astype(jnp.float32)
        moments[0:1, pl.ds(r * bs, bs)] = scales[0] * jnp.sum(base * base, axis=0, keepdims=True)
    for k in range(chunks):
        load(k).wait()
    finish_exchange(0)

    for k in range(chunks):
        def first_row(i, carry, k=k):
            r = k * part + i
            first = product(0, r).astype(jnp.bfloat16)
            own[1][r] = first
            gathered[1][g * rows + r] = first
            term = own[0][r].astype(jnp.float32) * first.astype(jnp.float32)
            moments[1:2, pl.ds(pl.multiple_of(r * bs, bs), bs)] = scales[1] * jnp.sum(term, axis=0, keepdims=True)
            return carry

        lax.fori_loop(0, part, first_row, 0, unroll=4)
        send_chunk(1, k)
    send_edges(1)
    finish_exchange(1)

    def second_row(r, carry):
        base = own[0][r].astype(jnp.float32)
        term = base * (2.0 * product(1, r) - base)
        moments[2:3, pl.ds(pl.multiple_of(r * bs, bs), bs)] = scales[2] * jnp.sum(term, axis=0, keepdims=True)
        return carry

    lax.fori_loop(0, rows, second_row, 0, unroll=4)
    drain(0)
    drain(1)


def solution(mesh):
    doms, lanes = mesh.shape["dom"], mesh.shape["grp"]

    def on_device(blocks, local_cols, remote_refs, send_blocks, send_counts, probes):
        count, nodes = probes.shape
        rows, _, bs, _ = blocks.shape
        cap = send_blocks.shape[3]
        norm = 1.0 / math.sqrt(count)
        scales = tuple((1.0 if k == 0 else 2.0) * jackson(k, KMOM) * norm for k in range(3))
        chunks = 4
        hops = lanes // 2 - 1
        dma = pltpu.SemaphoreType.DMA
        vmem = pl.BlockSpec(memory_space=pltpu.VMEM)
        smem = pl.BlockSpec(memory_space=pltpu.SMEM)
        return pl.pallas_call(
            functools.partial(kernel, doms, lanes, chunks, scales),
            out_shape=jax.ShapeDtypeStruct((3, nodes), jnp.float32),
            in_specs=[smem, smem, smem, smem, vmem, pl.BlockSpec(memory_space=pl.ANY)],
            out_specs=vmem,
            scratch_shapes=[
                pltpu.VMEM(blocks.shape, jnp.bfloat16),
                pltpu.VMEM((rows, count, bs), jnp.bfloat16),
                pltpu.VMEM((rows, count, bs), jnp.bfloat16),
                pltpu.VMEM((lanes * rows, count, bs), jnp.bfloat16),
                pltpu.VMEM((lanes * rows, count, bs), jnp.bfloat16),
                pltpu.VMEM((2, doms * cap, count, bs), jnp.bfloat16),
                pltpu.VMEM((doms * cap, count, bs), jnp.bfloat16),
                pltpu.VMEM((doms * cap, count, bs), jnp.bfloat16),
                dma((chunks,)),
                dma((2, hops, chunks)), dma((2, hops, chunks)),
                dma((2, chunks)), dma((2, chunks)),
                dma((2, hops, chunks)), dma((2, hops, chunks)),
                dma((2, doms)), dma((2, doms)),
            ],
            compiler_params=pltpu.CompilerParams(
                collective_id=0, has_side_effects=True, vmem_limit_bytes=48 * 2**20
            ),
        )(local_cols.T, remote_refs.T, send_blocks[0, 0].T, send_counts[0], probes, blocks)

    in_specs = (
        P(("dom", "grp"), None, None, None),
        P(("dom", "grp"), None),
        P(("dom", "grp"), None),
        P("dom", "grp", None, None),
        P("dom", "grp", None),
        P(None, ("dom", "grp")),
    )
    return jax.shard_map(
        on_device, mesh=mesh, in_specs=in_specs, out_specs=P(None, ("dom", "grp")), check_vma=False
    )
```

```python
import functools
import math

import jax
import jax.numpy as jnp
from jax import lax
from jax.experimental import pallas as pl
from jax.experimental.pallas import tpu as pltpu
from jax.sharding import PartitionSpec as P

KMOM = 256
UNROLL = 4
MESH = pl.DeviceIdType.MESH


def jackson(order, total):
    angle = math.pi / (total + 1)
    return (
        (total - order + 1) * math.cos(order * angle) + math.sin(order * angle) / math.tan(angle)
    ) / (total + 1)


def kernel(
    doms, lanes, chunks, halves, scales,
    cols_hbm, refs_hbm, blocks_sent, counts_sent, probes_hbm, blocks, moments,
    weights, probes, cols, refs, send_blocks, send_counts, *rest,
):
    stages = 2 * halves
    own, gathered, outgoing, received = (rest[i * stages : (i + 1) * stages] for i in range(4))
    (index_sem, probe_sem, load_sem, across_send, across_recv, pair_send, pair_recv,
     pass_send, pass_recv, edge_send, edge_recv) = rest[4 * stages :]
    rows, count, bs = own[0].shape
    local = cols.shape[0]
    remote = refs.shape[0]
    cap = send_blocks.shape[0]
    part = rows // chunks
    hops = lanes // 2 - 1
    d = lax.axis_index("dom")
    g = lax.axis_index("grp")
    pair = g + 1 - 2 * lax.rem(g, 2)

    def load(k):
        span = pl.ds(k * part, part)
        return pltpu.make_async_copy(blocks.at[span], weights.at[span], load_sem.at[k])

    def load_probes(k):
        span = pl.ds(k * part * bs, part * bs)
        return pltpu.make_async_copy(probes_hbm.at[:, span], probes.at[:, span], probe_sem.at[k])

    index_loads = [
        pltpu.make_async_copy(source, target, index_sem.at[i])
        for i, (source, target) in enumerate(
            ((blocks_sent, send_blocks), (counts_sent, send_counts), (cols_hbm, cols), (refs_hbm, refs))
        )
    ]
    for k in range(chunks):
        load_probes(k).start()
    for copy in index_loads:
        copy.start()

    barrier = pltpu.get_barrier_semaphore()
    for hop in range(1, lanes):
        pl.semaphore_signal(barrier, inc=1, device_id=(d, lax.rem(g + hop, lanes)), device_id_type=MESH)

    @pl.loop(1, doms)
    def _(k):
        pl.semaphore_signal(barrier, inc=1, device_id=(lax.rem(d + k, doms), g), device_id_type=MESH)

    def across(stage, hop, k):
        to = lax.rem(g + 2 * hop, lanes)
        return pltpu.make_async_remote_copy(
            own[stage].at[pl.ds(k * part, part)],
            gathered[stage].at[pl.ds(g * rows + k * part, part)],
            across_send.at[stage, hop - 1, k], across_recv.at[stage, hop - 1, k],
            device_id=(d, to), device_id_type=MESH,
        )

    def to_pair(stage, k):
        return pltpu.make_async_remote_copy(
            own[stage].at[pl.ds(k * part, part)],
            gathered[stage].at[pl.ds(g * rows + k * part, part)],
            pair_send.at[stage, k], pair_recv.at[stage, k],
            device_id=(d, pair), device_id_type=MESH,
        )

    def pass_on(stage, hop, k):
        origin = lax.rem(g - 2 * hop + lanes, lanes)
        span = pl.ds(origin * rows + k * part, part)
        return pltpu.make_async_remote_copy(
            gathered[stage].at[span], gathered[stage].at[span],
            pass_send.at[stage, hop - 1, k], pass_recv.at[stage, hop - 1, k],
            device_id=(d, pair), device_id_type=MESH,
        )

    def edge(stage, k):
        to = lax.rem(d + k, doms)
        return pltpu.make_async_remote_copy(
            outgoing[stage].at[pl.ds(to * cap, cap)],
            received[stage].at[pl.ds(d * cap, cap)],
            edge_send.at[stage, k], edge_recv.at[stage, k],
            device_id=(to, g), device_id_type=MESH,
        )

    def send_across(stage, k):
        for hop in range(1, hops + 1):
            across(stage, hop, k).start()

    def send_edges(stage):
        def packed(to, s):
            block = own[stage][send_blocks[s, 0, to]]
            return jnp.where(s < send_counts[0, 0, to], block, jnp.zeros_like(block))

        @pl.loop(1, doms)
        def _(k):
            to = lax.rem(d + k, doms)
            for s in range(cap):
                outgoing[stage][to * cap + s] = packed(to, s)
            edge(stage, k).start()

        for s in range(cap):
            received[stage][d * cap + s] = packed(d, s)

    def finish_exchange(stage):
        for k in range(chunks):
            for hop in range(1, hops + 1):
                across(stage, hop, k).wait_recv()
                pass_on(stage, hop, k).start()
        for k in range(chunks):
            to_pair(stage, k).wait_recv()

        @pl.loop(1, doms)
        def _(k):
            edge(stage, k).wait_recv()

        for k in range(chunks):
            for hop in range(1, hops + 1):
                pass_on(stage, hop, k).wait_recv()

    def drain(stage):
        for k in range(chunks):
            for hop in range(1, hops + 1):
                across(stage, hop, k).wait_send()
                pass_on(stage, hop, k).wait_send()
            to_pair(stage, k).wait_send()

        @pl.loop(1, doms)
        def _(k):
            edge(stage, k).wait_send()

    def product(stage, r):
        picked = [gathered[stage][cols[j, r]] for j in range(local)]
        picked += [received[stage][refs[j, r]] for j in range(remote)]
        held = [weights[r, j] for j in range(local + remote)]
        return lax.dot_general(
            jnp.concatenate(picked, axis=1), jnp.concatenate(held, axis=1),
            (((1,), (1,)), ((), ())), preferred_element_type=jnp.float32,
        )

    def add_moment(order, half, r, term):
        at = pl.ds(pl.multiple_of(r * bs, bs), bs)
        total = scales[order] * jnp.sum(term, axis=0, keepdims=True)
        if half > 0:
            total = moments[order : order + 1, at] + total
        moments[order : order + 1, at] = total

    for k in range(chunks):
        load_probes(k).wait()
        for half in range(halves):
            for r in range(k * part, (k + 1) * part):
                block = probes[half * count : (half + 1) * count, r * bs : (r + 1) * bs]
                own[half][r] = block
                gathered[half][g * rows + r] = block
        if k == 0:
            pl.semaphore_wait(barrier, lanes - 1 + doms - 1)
        send_across(0, k)
    for half in range(1, halves):
        for k in range(chunks):
            send_across(half, k)
    for half in range(halves):
        for k in range(chunks):
            to_pair(half, k).start()
    for copy in index_loads:
        copy.wait()
    for half in range(halves):
        send_edges(half)
    for k in range(chunks):
        load(k).start()

    for half in range(halves):
        def zeroth_row(r, carry, half=half):
            base = own[half][r].astype(jnp.float32)
            add_moment(0, half, r, base * base)
            return carry

        lax.fori_loop(0, rows, zeroth_row, 0, unroll=4)
    for k in range(chunks):
        load(k).wait()

    for half in range(halves):
        finish_exchange(half)
        for k in range(chunks):
            def first_row(i, carry, half=half, k=k):
                r = k * part + i
                first = product(half, r).astype(jnp.bfloat16)
                own[halves + half][r] = first
                gathered[halves + half][g * rows + r] = first
                add_moment(1, half, r, own[half][r].astype(jnp.float32) * first.astype(jnp.float32))
                return carry

            lax.fori_loop(0, part, first_row, 0, unroll=UNROLL)
            send_across(halves + half, k)
            to_pair(halves + half, k).start()
        send_edges(halves + half)

    for half in range(halves):
        finish_exchange(halves + half)

        def second_row(r, carry, half=half):
            base = own[half][r].astype(jnp.float32)
            add_moment(2, half, r, base * (2.0 * product(halves + half, r) - base))
            return carry

        lax.fori_loop(0, rows, second_row, 0, unroll=UNROLL)
    for stage in range(stages):
        drain(stage)


def solution(mesh):
    doms, lanes = mesh.shape["dom"], mesh.shape["grp"]

    def on_device(blocks, local_cols, remote_refs, send_blocks, send_counts, probes):
        count, nodes = probes.shape
        rows, _, bs, _ = blocks.shape
        cap = send_blocks.shape[3]
        norm = 1.0 / math.sqrt(count)
        scales = tuple((1.0 if k == 0 else 2.0) * jackson(k, KMOM) * norm for k in range(3))
        chunks, halves = 4, 2
        stages = 2 * halves
        hops = lanes // 2 - 1
        piece = (count // halves, bs)
        dma = pltpu.SemaphoreType.DMA
        hbm = pl.BlockSpec(memory_space=pltpu.HBM)
        operands = (
            local_cols.T, remote_refs.T, send_blocks[0].transpose(2, 0, 1), send_counts, probes, blocks
        )
        return pl.pallas_call(
            functools.partial(kernel, doms, lanes, chunks, halves, scales),
            out_shape=jax.ShapeDtypeStruct((3, nodes), jnp.float32),
            in_specs=[hbm] * 6,
            out_specs=pl.BlockSpec(memory_space=pltpu.VMEM),
            scratch_shapes=[
                pltpu.VMEM(blocks.shape, jnp.bfloat16),
                pltpu.VMEM(probes.shape, jnp.bfloat16),
                *(pltpu.SMEM(operand.shape, jnp.int32) for operand in operands[:4]),
                *[pltpu.VMEM((rows, *piece), jnp.bfloat16)] * stages,
                *[pltpu.VMEM((lanes * rows, *piece), jnp.bfloat16)] * stages,
                *[pltpu.VMEM((doms * cap, *piece), jnp.bfloat16)] * stages,
                *[pltpu.VMEM((doms * cap, *piece), jnp.bfloat16)] * stages,
                dma((4,)), dma((chunks,)), dma((chunks,)),
                dma((stages, hops, chunks)), dma((stages, hops, chunks)),
                dma((stages, chunks)), dma((stages, chunks)),
                dma((stages, hops, chunks)), dma((stages, hops, chunks)),
                dma((stages, doms)), dma((stages, doms)),
            ],
            compiler_params=pltpu.CompilerParams(
                collective_id=0, has_side_effects=True, vmem_limit_bytes=60 * 2**20
            ),
        )(*operands)

    in_specs = (
        P(("dom", "grp"), None, None, None),
        P(("dom", "grp"), None),
        P(("dom", "grp"), None),
        P("dom", "grp", None, None),
        P("dom", "grp", None),
        P(None, ("dom", "grp")),
    )
    return jax.shard_map(
        on_device, mesh=mesh, in_specs=in_specs, out_specs=P(None, ("dom", "grp")), check_vma=False
    )
```

```python
import functools
import math

import jax
import jax.numpy as jnp
from jax import lax
from jax.experimental import pallas as pl
from jax.experimental.pallas import tpu as pltpu
from jax.sharding import PartitionSpec as P

KMOM = 256
UNROLL = 12
MESH = pl.DeviceIdType.MESH


def jackson(order, total):
    angle = math.pi / (total + 1)
    return (
        (total - order + 1) * math.cos(order * angle) + math.sin(order * angle) / math.tan(angle)
    ) / (total + 1)


def kernel(
    doms, lanes, chunks, halves, scales,
    cols_hbm, refs_hbm, blocks_sent, counts_sent, probes_hbm, blocks, moments,
    weights, probes, cols, refs, send_blocks, send_counts, *rest,
):
    stages = 2 * halves
    own, gathered, outgoing, received = (rest[i * stages : (i + 1) * stages] for i in range(4))
    (index_sem, probe_sem, load_sem, across_send, across_recv, pair_send, pair_recv,
     pass_send, pass_recv, edge_send, edge_recv) = rest[4 * stages :]
    rows, count, bs = own[0].shape
    local = cols.shape[0]
    remote = refs.shape[0]
    cap = send_blocks.shape[0]
    part = rows // chunks
    hops = lanes // 2 - 1
    d = lax.axis_index("dom")
    g = lax.axis_index("grp")
    pair = g + 1 - 2 * lax.rem(g, 2)

    def load(k):
        span = pl.ds(k * part, part)
        return pltpu.make_async_copy(blocks.at[span], weights.at[span], load_sem.at[k])

    def load_probes(k):
        span = pl.ds(k * part * bs, part * bs)
        return pltpu.make_async_copy(probes_hbm.at[:, span], probes.at[:, span], probe_sem.at[k])

    index_loads = [
        pltpu.make_async_copy(source, target, index_sem.at[i])
        for i, (source, target) in enumerate(
            ((blocks_sent, send_blocks), (counts_sent, send_counts), (cols_hbm, cols), (refs_hbm, refs))
        )
    ]
    for k in range(chunks):
        load_probes(k).start()
    for copy in index_loads:
        copy.start()

    barrier = pltpu.get_barrier_semaphore()
    for hop in range(1, lanes):
        pl.semaphore_signal(barrier, inc=1, device_id=(d, lax.rem(g + hop, lanes)), device_id_type=MESH)

    @pl.loop(1, doms)
    def _(k):
        pl.semaphore_signal(barrier, inc=1, device_id=(lax.rem(d + k, doms), g), device_id_type=MESH)

    def across(stage, hop, k):
        to = lax.rem(g + 2 * hop, lanes)
        return pltpu.make_async_remote_copy(
            own[stage].at[pl.ds(k * part, part)],
            gathered[stage].at[pl.ds(g * rows + k * part, part)],
            across_send.at[stage, hop - 1, k], across_recv.at[stage, hop - 1, k],
            device_id=(d, to), device_id_type=MESH,
        )

    def to_pair(stage, k):
        return pltpu.make_async_remote_copy(
            own[stage].at[pl.ds(k * part, part)],
            gathered[stage].at[pl.ds(g * rows + k * part, part)],
            pair_send.at[stage, k], pair_recv.at[stage, k],
            device_id=(d, pair), device_id_type=MESH,
        )

    def pass_on(stage, hop, k):
        origin = lax.rem(g - 2 * hop + lanes, lanes)
        span = pl.ds(origin * rows + k * part, part)
        return pltpu.make_async_remote_copy(
            gathered[stage].at[span], gathered[stage].at[span],
            pass_send.at[stage, hop - 1, k], pass_recv.at[stage, hop - 1, k],
            device_id=(d, pair), device_id_type=MESH,
        )

    def edge(stage, k):
        to = lax.rem(d + k, doms)
        return pltpu.make_async_remote_copy(
            outgoing[stage].at[pl.ds(to * cap, cap)],
            received[stage].at[pl.ds(d * cap, cap)],
            edge_send.at[stage, k], edge_recv.at[stage, k],
            device_id=(to, g), device_id_type=MESH,
        )

    def send_edges(stage):
        def packed(to, s):
            block = own[stage][send_blocks[s, 0, to]]
            return jnp.where(s < send_counts[0, 0, to], block, jnp.zeros_like(block))

        @pl.loop(1, doms)
        def _(k):
            to = lax.rem(d + k, doms)
            for s in range(cap):
                outgoing[stage][to * cap + s] = packed(to, s)
            edge(stage, k).start()

        for s in range(cap):
            received[stage][d * cap + s] = packed(d, s)

    def advance(stage, k):
        for hop in range(1, hops + 1):
            across(stage, hop, k).wait_send()
            if stage + 1 < stages:
                across(stage + 1, hop, k).start()
        for hop in range(1, hops + 1):
            across(stage, hop, k).wait_recv()
            pass_on(stage, hop, k).start()

    def finish_exchange(stage):
        for k in range(chunks):
            to_pair(stage, k).wait_recv()

        @pl.loop(1, doms)
        def _(k):
            edge(stage, k).wait_recv()

        for k in range(chunks):
            for hop in range(1, hops + 1):
                pass_on(stage, hop, k).wait_recv()

    def drain(stage):
        for k in range(chunks):
            for hop in range(1, hops + 1):
                pass_on(stage, hop, k).wait_send()
            to_pair(stage, k).wait_send()

        @pl.loop(1, doms)
        def _(k):
            edge(stage, k).wait_send()

    def product(stage, r):
        picked = [gathered[stage][cols[j, r]] for j in range(local)]
        picked += [received[stage][refs[j, r]] for j in range(remote)]
        held = [weights[r, j] for j in range(local + remote)]
        return lax.dot_general(
            jnp.concatenate(picked, axis=1), jnp.concatenate(held, axis=1),
            (((1,), (1,)), ((), ())), preferred_element_type=jnp.float32,
        )

    def add_moment(order, half, r, term):
        at = pl.ds(pl.multiple_of(r * bs, bs), bs)
        total = scales[order] * jnp.sum(term, axis=0, keepdims=True)
        if half > 0:
            total = moments[order : order + 1, at] + total
        moments[order : order + 1, at] = total

    for k in range(chunks):
        load_probes(k).wait()
        for half in range(halves):
            for r in range(k * part, (k + 1) * part):
                block = probes[half * count : (half + 1) * count, r * bs : (r + 1) * bs]
                own[half][r] = block
                gathered[half][g * rows + r] = block
        if k == 0:
            pl.semaphore_wait(barrier, lanes - 1 + doms - 1)
        for hop in range(1, hops + 1):
            across(0, hop, k).start()
    for half in range(halves):
        for k in range(chunks):
            to_pair(half, k).start()
    for copy in index_loads:
        copy.wait()
    for half in range(halves):
        send_edges(half)
    for k in range(chunks):
        load(k).start()

    for half in range(halves):
        def zeroth_row(r, carry, half=half):
            base = own[half][r].astype(jnp.float32)
            add_moment(0, half, r, base * base)
            return carry

        lax.fori_loop(0, rows, zeroth_row, 0, unroll=4)
    for k in range(chunks):
        load(k).wait()
    for k in range(chunks):
        advance(0, k)

    for half in range(halves):
        finish_exchange(half)
        for k in range(chunks):
            def first_row(i, carry, half=half, k=k):
                r = k * part + i
                first = product(half, r).astype(jnp.bfloat16)
                own[halves + half][r] = first
                gathered[halves + half][g * rows + r] = first
                add_moment(1, half, r, own[half][r].astype(jnp.float32) * first.astype(jnp.float32))
                return carry

            lax.fori_loop(0, part, first_row, 0, unroll=UNROLL)
            to_pair(halves + half, k).start()
            advance(half + 1, k)
        send_edges(halves + half)

    for half in range(halves):
        finish_exchange(halves + half)

        def second_row(r, carry, half=half):
            base = own[half][r].astype(jnp.float32)
            add_moment(2, half, r, base * (2.0 * product(halves + half, r) - base))
            return carry

        for k in range(chunks):
            lax.fori_loop(k * part, (k + 1) * part, second_row, 0, unroll=UNROLL)
            if half + 1 < halves:
                advance(halves + half + 1, k)
    for stage in range(stages):
        drain(stage)


def solution(mesh):
    doms, lanes = mesh.shape["dom"], mesh.shape["grp"]

    def on_device(blocks, local_cols, remote_refs, send_blocks, send_counts, probes):
        count, nodes = probes.shape
        rows, _, bs, _ = blocks.shape
        cap = send_blocks.shape[3]
        norm = 1.0 / math.sqrt(count)
        scales = tuple((1.0 if k == 0 else 2.0) * jackson(k, KMOM) * norm for k in range(3))
        chunks, halves = 4, 2
        stages = 2 * halves
        hops = lanes // 2 - 1
        piece = (count // halves, bs)
        dma = pltpu.SemaphoreType.DMA
        hbm = pl.BlockSpec(memory_space=pltpu.HBM)
        operands = (
            local_cols.T, remote_refs.T, send_blocks[0].transpose(2, 0, 1), send_counts, probes, blocks
        )
        return pl.pallas_call(
            functools.partial(kernel, doms, lanes, chunks, halves, scales),
            out_shape=jax.ShapeDtypeStruct((3, nodes), jnp.float32),
            in_specs=[hbm] * 6,
            out_specs=pl.BlockSpec(memory_space=pltpu.VMEM),
            scratch_shapes=[
                pltpu.VMEM(blocks.shape, jnp.bfloat16),
                pltpu.VMEM(probes.shape, jnp.bfloat16),
                *(pltpu.SMEM(operand.shape, jnp.int32) for operand in operands[:4]),
                *[pltpu.VMEM((rows, *piece), jnp.bfloat16)] * stages,
                *[pltpu.VMEM((lanes * rows, *piece), jnp.bfloat16)] * stages,
                *[pltpu.VMEM((doms * cap, *piece), jnp.bfloat16)] * stages,
                *[pltpu.VMEM((doms * cap, *piece), jnp.bfloat16)] * stages,
                dma((4,)), dma((chunks,)), dma((chunks,)),
                dma((stages, hops, chunks)), dma((stages, hops, chunks)),
                dma((stages, chunks)), dma((stages, chunks)),
                dma((stages, hops, chunks)), dma((stages, hops, chunks)),
                dma((stages, doms)), dma((stages, doms)),
            ],
            compiler_params=pltpu.CompilerParams(
                collective_id=0, has_side_effects=True, vmem_limit_bytes=60 * 2**20
            ),
        )(*operands)

    in_specs = (
        P(("dom", "grp"), None, None, None),
        P(("dom", "grp"), None),
        P(("dom", "grp"), None),
        P("dom", "grp", None, None),
        P("dom", "grp", None),
        P(None, ("dom", "grp")),
    )
    return jax.shard_map(
        on_device, mesh=mesh, in_specs=in_specs, out_specs=P(None, ("dom", "grp")), check_vma=False
    )
```
